32 devices in a mesh: grp: 2 (over x), tm: 16 (over z, y, core).
Axes of the slice: x: 2, y: 2, z: 4, core: 2. Of those that a mesh axis runs over, the one named last changes fastest.
Arguments:
- density: float32 [32, 512, 512], P(('grp', 'tm')), parts along dimension 0, may hold values from 0.25 to 2.5
- flux_x: float32 [32, 512, 512], P(('grp', 'tm')), parts along dimension 0, may hold values from -5 to 5
- flux_y: float32 [32, 512, 512], P(('grp', 'tm')), parts along dimension 0, may hold values from -5 to 5
- potential: float32 [32, 512, 512], P(('grp', 'tm')), parts along dimension 0, may hold values from -6 to 6
- initial_density: float32 [1024, 512], P('grp'), parts along dimension 0, may hold values from 0.25 to 2.5
- running_cost: float32 [1024, 512], P('grp'), parts along dimension 0, may hold values from 0 to 1.5
Outputs:
- density_out: float32 [32, 512, 512], P(('grp', 'tm')), parts along dimension 0
- flux_x_out: float32 [32, 512, 512], P(('grp', 'tm')), parts along dimension 0
- flux_y_out: float32 [32, 512, 512], P(('grp', 'tm')), parts along dimension 0
- potential_out: float32 [32, 512, 512], P(('grp', 'tm')), parts along dimension 0
The draws below stay inside these ranges and needn't reach their ends.
There are 2 independent parts, one for each index of `grp`. The reference program is written for one: setup_inputs(seed, part) draws one part's arguments, and reference() takes and returns one part's arrays. A program takes and returns all parts, laid end to end along the dimension named above; each array names one. Nothing has to cross between parts.
All inputs are finite; a program needn't handle non-finite values.
Results may differ from the reference program's by a relative error of at most 0.00018.
Values sent between devices are 32-bit elements; how exact they have to be, the bound alone decides.
A program may use at most 64 MiB of HBM per device.

```python
import math
import jax
import jax.numpy as jnp
from jax import lax

NX = 512
NY = 512
ITERS = 2
NEWTON = 3
TIME = 16


def block_levels(stream_key, shape, cuts, least, largest):
    loudness, own = 1.0, jax.random.fold_in(stream_key, 6)
    for dim, parts in cuts:
        heights = jnp.exp(jax.random.uniform(jax.random.fold_in(own, dim), (parts,), jnp.float32, least / len(cuts), largest / len(cuts)))
        loudness = loudness * jnp.repeat(heights, shape[dim] // parts).reshape([-1 if axis == dim else 1 for axis in range(len(shape))])
    return loudness


def centred(stream_key, dims, deviation, limit, shards=(), held_as=jnp.bfloat16):
    loudness = block_levels(stream_key, dims, shards, -0.22, 0.18) if shards else 1.0
    result = jax.random.normal(stream_key, dims, jnp.float32) * deviation * loudness
    return jnp.minimum(jnp.maximum(result, -limit), limit).astype(held_as)


def setup_inputs(seed: int = 0, part: int = 0) -> dict:
    key_list = jax.random.split(jax.random.key(seed), 7)
    own_keys = jax.random.split(jax.random.fold_in(key_list[6], part), 7)
    return {
        "density": jnp.clip(jnp.exp(math.log(2.5) - 2.3025851 * jax.random.uniform(own_keys[0], (TIME, NX, NY), jnp.float32) ** block_levels(own_keys[0], (TIME, NX, NY), ((0, 16),), -0.2, 0.2)), 0.25, 2.5),
        "flux_x": centred(own_keys[1], (TIME, NX, NY), 0.7, 5.0, ((0, 16),), jnp.float32),
        "flux_y": centred(own_keys[2], (TIME, NX, NY), 0.7, 5.0, ((0, 16),), jnp.float32),
        "potential": centred(own_keys[3], (TIME, NX, NY), 1.0, 6.0, ((0, 16),), jnp.float32),
        "initial_density": jnp.clip(jnp.exp(jax.random.uniform(own_keys[4], (NX, NY), jnp.float32, math.log(0.25), math.log(2.5))), 0.25, 2.5),
        "running_cost": jnp.clip(jax.random.uniform(own_keys[5], (NX, NY), jnp.float32, 0.0, 1.5), 0.0, 1.5),
    }


PRIMAL_STEP = 0.5
DUAL_STEP = 0.5
CONGESTION = 0.1
SCREENING = 0.05

def cosine_table(length):
    freq = jnp.arange(length, dtype=jnp.float32)[:, None]
    place = jnp.arange(length, dtype=jnp.float32)[None, :]
    scale = jnp.where(freq == 0, jnp.sqrt(1.0 / length), jnp.sqrt(2.0 / length))
    return scale * jnp.cos(jnp.pi * (place + 0.5) * freq / length)

def spectrum(length):
    return 2.0 - 2.0 * jnp.cos(jnp.pi * jnp.arange(length, dtype=jnp.float32) / length)

def forward_diff(values, dimension):
    differences = jnp.diff(values, axis=dimension)
    widths = [(0, 0), (0, 0), (0, 0)]
    widths[dimension] = (0, 1)
    return jnp.pad(differences, widths)

def backward_div(flux_part, dimension):
    count = flux_part.shape[dimension]
    kept = lax.slice_in_dim(flux_part, 0, count - 1, axis=dimension)
    after = [(0, 0), (0, 0), (0, 0)]
    after[dimension] = (0, 1)
    before = [(0, 0), (0, 0), (0, 0)]
    before[dimension] = (1, 0)
    return jnp.pad(kept, after) - jnp.pad(kept, before)

def proximal(density, flux_x, flux_y, time_grad, grad_x, grad_y, running_cost):
    moment_x = flux_x + PRIMAL_STEP * grad_x
    moment_y = flux_y + PRIMAL_STEP * grad_y
    kinetic = 0.5 * PRIMAL_STEP * (moment_x * moment_x + moment_y * moment_y)
    slope = 1.0 + CONGESTION * PRIMAL_STEP
    offset = density + PRIMAL_STEP * (time_grad - running_cost)
    guess = jnp.maximum(offset / slope, 0.0) + jnp.cbrt(kinetic / slope)
    for sweep in range(NEWTON):
        shifted = guess + PRIMAL_STEP
        linear = slope * guess - offset
        residue = linear * shifted * shifted - kinetic
        derivative = slope * shifted * shifted + 2.0 * linear * shifted
        guess = jnp.maximum(guess - residue / derivative, 0.0)
    weight = guess / (guess + PRIMAL_STEP)
    return (guess, weight * moment_x, weight * moment_y)

def reference(density, flux_x, flux_y, potential, initial_density, running_cost):
    times, rows_all, cols_all = density.shape
    table_t = cosine_table(times)
    table_x = cosine_table(rows_all)
    table_y = cosine_table(cols_all)
    denominator = SCREENING + spectrum(times)[:, None, None] + spectrum(rows_all)[None, :, None] + spectrum(cols_all)[None, None, :]
    highest = lax.Precision.HIGHEST
    for sweep in range(ITERS):
        time_grad = forward_diff(potential, 0)
        grad_x = forward_diff(potential, 1)
        grad_y = forward_diff(potential, 2)
        new_density, new_x, new_y = proximal(density, flux_x, flux_y, time_grad, grad_x, grad_y, running_cost[None])
        bar_density = 2.0 * new_density - density
        bar_x = 2.0 * new_x - flux_x
        bar_y = 2.0 * new_y - flux_y
        previous = jnp.concatenate([initial_density[None], bar_density[:-1]], axis=0)
        source = bar_density - previous + backward_div(bar_x, 1) + backward_div(bar_y, 2)
        modes = jnp.einsum('ax,txy->tay', table_x, source, precision=highest)
        modes = jnp.einsum('txy,by->txb', modes, table_y, precision=highest)
        modes = jnp.einsum('kt,txy->kxy', table_t, modes, precision=highest)
        modes = modes / denominator
        field = jnp.einsum('kt,kxy->txy', table_t, modes, precision=highest)
        field = jnp.einsum('ax,tay->txy', table_x, field, precision=highest)
        field = jnp.einsum('txb,by->txy', field, table_y, precision=highest)
        potential = potential + DUAL_STEP * field
        density, flux_x, flux_y = (new_density, new_x, new_y)
    return (density, flux_x, flux_y, potential)
```

```python
import functools

import jax
import jax.numpy as jnp
import ml_dtypes
import numpy as np
from jax import lax
from jax.experimental import pallas as pl
from jax.experimental.pallas import tpu as pltpu
from jax.sharding import PartitionSpec as P

NEWTON = 3

PRIMAL_STEP = 0.5
DUAL_STEP = 0.5
CONGESTION = 0.1
SCREENING = 0.05

CHUNKS = 4
TILE = 32
VMEM_BYTES = 56 * 1024 * 1024
F32 = jnp.float32
BF16 = jnp.bfloat16


def cosine_table(length):
    freq = np.arange(length, dtype=np.float64)[:, None]
    place = np.arange(length, dtype=np.float64)[None, :]
    scale = np.where(freq == 0, np.sqrt(1.0 / length), np.sqrt(2.0 / length))
    return scale * np.cos(np.pi * (place + 0.5) * freq / length)


def spectrum(length):
    return 2.0 - 2.0 * np.cos(np.pi * np.arange(length, dtype=np.float64) / length)


def halves(table):
    high = table.astype(np.float32).astype(ml_dtypes.bfloat16)
    low = (table - high.astype(np.float64)).astype(np.float32).astype(ml_dtypes.bfloat16)
    return np.stack([high, low])


def split(value):
    high = value.astype(BF16)
    return high, (value - high.astype(F32)).astype(BF16)


def product(a_high, a_low, b_high, b_low):
    dot = functools.partial(jnp.dot, preferred_element_type=F32)
    return dot(a_high, b_high) + (dot(a_low, b_high) + dot(a_high, b_low))


def two_sided(read, left, right, mid, write, rows):
    step = min(256, rows)
    for r0 in range(0, rows, step):
        high, low = split(read(r0, step))
        high, low = split(product(high, low, right[0], right[1]))
        mid[0, r0 : r0 + step, :] = high
        mid[1, r0 : r0 + step, :] = low
    for r0 in range(0, rows, step):
        here = slice(r0, r0 + step)
        write(r0, step, product(left[0, here, :], left[1, here, :], mid[0], mid[1]))


def proximal(density, flux_x, flux_y, time_grad, grad_x, grad_y, running_cost):
    moment_x = flux_x + PRIMAL_STEP * grad_x
    moment_y = flux_y + PRIMAL_STEP * grad_y
    kinetic = 0.5 * PRIMAL_STEP * (moment_x * moment_x + moment_y * moment_y)
    slope = 1.0 + CONGESTION * PRIMAL_STEP
    offset = density + PRIMAL_STEP * (time_grad - running_cost)
    root = jnp.exp2(jnp.log2(kinetic * (1.0 / slope)) * (1.0 / 3.0))
    guess = jnp.maximum(offset * (1.0 / slope), 0.0) + root
    for sweep in range(NEWTON):
        shifted = guess + PRIMAL_STEP
        linear = slope * guess - offset
        residue = linear * shifted * shifted - kinetic
        derivative = slope * shifted * shifted + 2.0 * linear * shifted
        guess = jnp.maximum(guess - residue / derivative, 0.0)
    weight = guess / (guess + PRIMAL_STEP)
    return (guess, weight * moment_x, weight * moment_y)


def forward_half(flag, fields, pot, following, cost, init, table_x, table_yt, outs, hat, work, mid):
    density, flux_x, flux_y = fields
    rows, cols = pot.shape
    first = flag[0] == 1
    last = flag[1] == 1

    def tile(index, carry):
        r0 = pl.multiple_of(index * TILE, TILE)
        here = pl.ds(r0, TILE)
        row = lax.broadcasted_iota(jnp.int32, (TILE, cols), 0)
        col = lax.broadcasted_iota(jnp.int32, (TILE, cols), 1)
        p = pot[here, :]
        below = pl.multiple_of(jnp.minimum(r0 + TILE, rows - 8), 8)
        edge = pot[pl.ds(below, 8), :][0:1, :]
        p_down = jnp.where(row == TILE - 1, edge, pltpu.roll(p, TILE - 1, 0))
        grad_x = jnp.where(row + r0 == rows - 1, 0.0, p_down - p)
        grad_y = jnp.where(col == cols - 1, 0.0, pltpu.roll(p, cols - 1, 1) - p)
        time_grad = jnp.where(last, 0.0, following[here, :] - p)
        old, old_x, old_y = density[here, :], flux_x[here, :], flux_y[here, :]
        new, new_x, new_y = proximal(old, old_x, old_y, time_grad, grad_x, grad_y, cost[here, :])
        outs[0][here, :] = new
        outs[1][here, :] = new_x
        outs[2][here, :] = new_y
        bar = 2.0 * new - old
        bar_x = 2.0 * new_x - old_x
        bar_y = jnp.where(col == cols - 1, 0.0, 2.0 * new_y - old_y)
        div_y = bar_y - jnp.where(col == 0, 0.0, pltpu.roll(bar_y, 1, 1))
        bar_x = jnp.where(row + r0 == rows - 1, 0.0, bar_x)
        before = jnp.where(row == 0, carry, pltpu.roll(bar_x, 1, 0))
        start = jnp.where(first, init[here, :], 0.0)
        work[1, here, :] = bar
        work[0, here, :] = bar - start + div_y + (bar_x - before)
        return bar_x[TILE - 1 : TILE, :]

    lax.fori_loop(0, rows // TILE, tile, jnp.zeros((1, cols), F32))

    for part in range(2):
        def read(r0, step):
            return work[part, r0 : r0 + step, :]

        def write(r0, step, value):
            hat[part, r0 : r0 + step, :] = value

        two_sided(read, table_x, table_yt, mid, write, rows)


def backward_half(modes, part, pot, table_xt, table_y, out, mid):
    def read(r0, step):
        return modes[part, r0 : r0 + step, :]

    def write(r0, step, value):
        here = slice(r0, r0 + step)
        out[here, :] = pot[here, :] + DUAL_STEP * value

    two_sided(read, table_xt, table_y, mid, write, pot.shape[0])


def first_kernel(flag, density, flux_x, flux_y, pot, following, cost, init, tx, tyt, o_d, o_x, o_y, hat, work, mid):
    forward_half(flag, (density, flux_x, flux_y), pot, following, cost, init, tx, tyt, (o_d, o_x, o_y), hat, work, mid)


def middle_kernel(
    flag, modes, density, flux_x, flux_y, pot, following, cost, init, tx, txt, ty, tyt,
    o_d, o_x, o_y, o_p, hat, work, mid, moved,
):
    backward_half(modes, 0, pot, txt, ty, o_p, mid)
    backward_half(modes, 1, following, txt, ty, moved, mid)
    forward_half(flag, (density, flux_x, flux_y), o_p, moved, cost, init, tx, tyt, (o_d, o_x, o_y), hat, work, mid)


def last_kernel(modes, pot, txt, ty, o_p, mid):
    backward_half(modes, 0, pot, txt, ty, o_p, mid)


def solve_kernel(
    n, wd, coef, other, x, wd_in, ab_out, ab_in, ab_own, p_in, p_out, q_in, q_out, give, got, own, x_out,
    core_s, core_r, y_s, y_r, p_s, p_r, q_s, q_r, ret_s, ret_r, x_s, x_r,
):
    me = lax.axis_index("tm")
    core = lax.rem(me, 2)
    side = lax.rem(me // 2, 2)
    g = me // 4
    groups = n // 4
    mate = me + 1 - 2 * core
    across = me + 2 - 4 * side
    ahead, behind = me + 4, me - 4
    half = wd.shape[1] // 2
    quarter = half // 2
    rows = quarter // CHUNKS
    cols = wd.shape[2]

    barrier = pltpu.get_barrier_semaphore()
    pl.semaphore_signal(barrier, inc=1, device_id={"tm": mate}, device_id_type=pl.DeviceIdType.MESH)
    pl.semaphore_signal(barrier, inc=1, device_id={"tm": across}, device_id_type=pl.DeviceIdType.MESH)

    @pl.when(g > 0)
    def _():
        pl.semaphore_signal(barrier, inc=1, device_id={"tm": behind}, device_id_type=pl.DeviceIdType.MESH)

    @pl.when(g < groups - 1)
    def _():
        pl.semaphore_signal(barrier, inc=1, device_id={"tm": ahead}, device_id_type=pl.DeviceIdType.MESH)

    @pl.when(g == 0)
    def _():
        p_in[...] = jnp.zeros_like(p_in)

    @pl.when(g == groups - 1)
    def _():
        q_in[...] = jnp.zeros_like(q_in)

    peers = 2 + (g > 0).astype(jnp.int32) + (g < groups - 1).astype(jnp.int32)
    pl.semaphore_wait(barrier, peers)

    def remote(src, dst, send, recv, target):
        return pltpu.make_async_remote_copy(
            src_ref=src, dst_ref=dst, send_sem=send, recv_sem=recv,
            device_id={"tm": target}, device_id_type=pl.DeviceIdType.MESH,
        )

    def at(k):
        return pl.ds(pl.multiple_of(k * rows, rows), rows)

    def in_half(k):
        part = jnp.where(k < CHUNKS, 1 - side, side)
        return pl.multiple_of(part * quarter + lax.rem(k, CHUNKS) * rows, rows)

    def core_copy(k):
        src = wd.at[:, pl.ds(pl.multiple_of((1 - core) * half + in_half(k), rows), rows), :]
        return remote(src, wd_in.at[:, pl.ds(in_half(k), rows), :], core_s.at[k], core_r.at[k], mate)

    def y_copy(k):
        return remote(ab_out.at[:, at(k), :], ab_in.at[:, at(k), :], y_s.at[k], y_r.at[k], across)

    def p_copy(k):
        return remote(p_out.at[at(k), :], p_in.at[at(k), :], p_s.at[k], p_r.at[k], ahead)

    def q_copy(k):
        return remote(q_out.at[at(k), :], q_in.at[at(k), :], q_s.at[k], q_r.at[k], behind)

    def ret_copy(part, k):
        return remote(give.at[part, at(k), :], got.at[part, at(k), :], ret_s.at[part, k], ret_r.at[part, k], across)

    def x_copy(k):
        here = pl.ds(in_half(k), rows)
        there = pl.ds(pl.multiple_of(core * half + in_half(k), rows), rows)
        return remote(x_out.at[:, here, :], x.at[:, there, :], x_s.at[k], x_r.at[k], mate)

    def loop(count, body):
        lax.fori_loop(0, count, lambda k, c: (body(k), c)[1], 0)

    loop(2 * CHUNKS, lambda k: core_copy(k).start())

    low = core == 0

    def sources(k):
        here = pl.ds(in_half(k), rows)
        mine = pl.ds(pl.multiple_of(core * half + in_half(k), rows), rows)
        w_a, d_a = wd[0, mine, :], wd[1, mine, :]
        w_b, d_b = wd_in[0, here, :], wd_in[1, here, :]
        w0 = jnp.where(low, w_a, w_b)
        s1 = jnp.where(low, w_b - d_a, w_a - d_b)
        d1 = jnp.where(low, d_b, d_a)
        return w0, s1, d1, [coef[j, here, :] for j in range(6)]

    def carries(k):
        w0, s1, d1, (f0, f1, h0, h1, h2, _) = sources(k)
        return f1 * (s1 + f0 * w0) - d1, h0 * (w0 + h1 * (s1 - h2 * d1))

    def out_chunk(k):
        core_copy(k).wait_recv()
        a, b = carries(k)
        ab_out[0, at(k), :] = a
        ab_out[1, at(k), :] = b
        y_copy(k).start()

    loop(CHUNKS, out_chunk)

    def own_chunk(k):
        core_copy(k + CHUNKS).wait_recv()
        a, b = carries(k + CHUNKS)
        ab_own[0, at(k), :] = a
        ab_own[1, at(k), :] = b

    loop(CHUNKS, own_chunk)

    left = side == 0

    def ordered(part, k, first, second):
        here = pl.ds(in_half(k + CHUNKS), rows)
        mine, theirs = ab_own[part, at(k), :], ab_in[part, at(k), :]
        rate, rate_other = coef[first, here, :] * coef[second, here, :], other[part, at(k), :]
        return (
            jnp.where(left, mine, theirs), jnp.where(left, rate, rate_other),
            jnp.where(left, theirs, mine), jnp.where(left, rate_other, rate),
        )

    def step(s):
        @pl.when(s < CHUNKS)
        def _():
            y_copy(s).wait_recv()

        kp = s - g

        @pl.when((kp >= 0) & (kp < CHUNKS))
        def _():
            @pl.when(g > 0)
            def _():
                p_copy(kp).wait_recv()

            a0, r0, a1, r1 = ordered(0, kp, 0, 1)
            enter = p_in[at(kp), :]
            middle = a0 + r0 * enter

            @pl.when(g < groups - 1)
            def _():
                p_out[at(kp), :] = a1 + r1 * middle
                p_copy(kp).start()

            own[0, at(kp), :] = jnp.where(left, enter, middle)
            give[0, at(kp), :] = jnp.where(left, middle, enter)
            ret_copy(0, kp).start()

        kq = s - (groups - 1 - g)

        @pl.when((kq >= 0) & (kq < CHUNKS))
        def _():
            @pl.when(g < groups - 1)
            def _():
                q_copy(kq).wait_recv()

            b0, r0, b1, r1 = ordered(1, kq, 2, 3)
            enter = q_in[at(kq), :]
            middle = b1 + r1 * enter

            @pl.when(g > 0)
            def _():
                q_out[at(kq), :] = b0 + r0 * middle
                q_copy(kq).start()

            own[1, at(kq), :] = jnp.where(left, middle, enter)
            give[1, at(kq), :] = jnp.where(left, enter, middle)
            ret_copy(1, kq).start()

    loop(CHUNKS + groups - 1, step)

    def finish(k, carry_p, carry_q):
        w0, s1, d1, (f0, f1, h0, h1, h2, g0) = sources(k)
        q2 = carry_q - h2 * d1
        q1 = h1 * (s1 + q2)
        x0 = (w0 + carry_p + q1) * g0
        x1 = h1 * x0 + q1
        x2 = h2 * x1 + q2
        here = pl.ds(in_half(k), rows)
        mine = pl.ds(pl.multiple_of(core * half + in_half(k), rows), rows)
        x[0, mine, :] = jnp.where(low, x0, x1)
        x[1, mine, :] = jnp.where(low, x1, x2)
        x_out[0, here, :] = jnp.where(low, x1, x0)
        x_out[1, here, :] = jnp.where(low, x2, x1)
        x_copy(k).start()

    loop(CHUNKS, lambda k: finish(k + CHUNKS, own[0, at(k), :], own[1, at(k), :]))

    def returned(k):
        ret_copy(0, k).wait_recv()
        ret_copy(1, k).wait_recv()
        finish(k, got[0, at(k), :], got[1, at(k), :])

    loop(CHUNKS, returned)

    def drain(k):
        core_copy(k).wait_send()
        x_copy(k).wait_send()
        x_copy(k).wait_recv()

    loop(2 * CHUNKS, drain)

    def drain_more(k):
        y_copy(k).wait_send()
        ret_copy(0, k).wait_send()
        ret_copy(1, k).wait_send()

        @pl.when(g < groups - 1)
        def _():
            p_copy(k).wait_send()

        @pl.when(g > 0)
        def _():
            q_copy(k).wait_send()

    loop(CHUNKS, drain_more)


def vmem(count):
    return [pl.BlockSpec(memory_space=pltpu.VMEM)] * count


def local_call(kernel, inputs, outs, scratch, flag=None):
    specs = vmem(len(inputs))
    if flag is not None:
        specs = [pl.BlockSpec(memory_space=pltpu.SMEM)] + specs
        inputs = [flag] + inputs
    return pl.pallas_call(
        kernel,
        out_shape=[jax.ShapeDtypeStruct(shape, F32) for shape in outs],
        in_specs=specs,
        out_specs=vmem(len(outs)),
        scratch_shapes=scratch,
        compiler_params=pltpu.CompilerParams(vmem_limit_bytes=VMEM_BYTES),
    )(*inputs)


def solve(n, wd, coef, other):
    _, rows, cols = wd.shape
    half, quarter = rows // 2, rows // 4
    dma = pltpu.SemaphoreType.DMA
    two = pltpu.VMEM((2, quarter, cols), F32)
    one = pltpu.VMEM((quarter, cols), F32)
    return pl.pallas_call(
        functools.partial(solve_kernel, n),
        out_shape=jax.ShapeDtypeStruct((2, rows, cols), F32),
        in_specs=vmem(3),
        out_specs=pl.BlockSpec(memory_space=pltpu.VMEM),
        scratch_shapes=[
            pltpu.VMEM((2, half, cols), F32), two, two, two, one, one, one, one, two, two, two,
            pltpu.VMEM((2, half, cols), F32),
            dma((2 * CHUNKS,)), dma((2 * CHUNKS,)), dma((CHUNKS,)), dma((CHUNKS,)),
            dma((CHUNKS,)), dma((CHUNKS,)), dma((CHUNKS,)), dma((CHUNKS,)),
            dma((2, CHUNKS)), dma((2, CHUNKS)), dma((2 * CHUNKS,)), dma((2 * CHUNKS,)),
        ],
        compiler_params=pltpu.CompilerParams(
            vmem_limit_bytes=VMEM_BYTES, collective_id=0, has_side_effects=True
        ),
    )(wd, coef, other)


def time_factors(n, position, rows, cols):
    lam_x = jnp.asarray(spectrum(rows), F32)
    lam_y = jnp.asarray(spectrum(cols), F32)
    half, quarter = rows // 2, rows // 4
    core, side, chip = position % 2, (position // 2) % 2, position // 2

    def pivots(start, count):
        mu = SCREENING + lax.dynamic_slice_in_dim(lam_x, start, count)[:, None] + lam_y[None, :]
        r = 2.0 / (mu + 2.0 + jnp.sqrt(mu * (mu + 4.0)))
        log_r = jnp.log(r)

        def inverse(i):
            power = jnp.exp(log_r * (2 * i + 1).astype(F32))
            return r * (1.0 + power) / (1.0 + power * r * r)

        return mu, inverse

    mu, inverse = pivots(core * half, half)
    i0 = 2 * chip
    h1 = inverse(n - 2 - i0)
    h2 = jnp.where(i0 + 2 == n, 0.0, inverse(jnp.maximum(n - 3 - i0, 0)))
    g0 = 1.0 / (mu + 2.0 - inverse(i0 - 1) - h1)
    coef = jnp.stack([inverse(i0), inverse(i0 + 1), inverse(n - 1 - i0), h1, h2, g0])
    _, inverse = pivots(core * half + side * quarter, quarter)
    j0 = 2 * (chip + 1 - 2 * side)
    other = jnp.stack([inverse(j0) * inverse(j0 + 1), inverse(n - 1 - j0) * inverse(n - 2 - j0)])
    return coef, other


def local(density, flux_x, flux_y, potential, initial_density, running_cost):
    n = lax.axis_size("tm")
    position = lax.axis_index("tm")
    _, rows, cols = density.shape
    shape = (rows, cols)
    following = lax.ppermute(potential[0], "tm", [(t, t - 1) for t in range(1, n)])
    coef, other = time_factors(n, position, rows, cols)
    flag = jnp.stack([position == 0, position == n - 1]).astype(jnp.int32)
    tx, ty = cosine_table(rows), cosine_table(cols)
    table_x, table_xt = jnp.asarray(halves(tx)), jnp.asarray(halves(tx.T))
    table_y, table_yt = jnp.asarray(halves(ty)), jnp.asarray(halves(ty.T))
    work = pltpu.VMEM((2, rows, cols), F32)
    mid = pltpu.VMEM((2, rows, cols), BF16)
    three = [shape] * 3
    hat_shape = (2, rows, cols)

    d, fx, fy, hat = local_call(
        first_kernel,
        [density[0], flux_x[0], flux_y[0], potential[0], following, running_cost, initial_density, table_x, table_yt],
        three + [hat_shape], [work, mid], flag,
    )
    modes = solve(n, hat, coef, other)
    d, fx, fy, pot, hat = local_call(
        middle_kernel,
        [modes, d, fx, fy, potential[0], following, running_cost, initial_density, table_x, table_xt, table_y, table_yt],
        three + [shape, hat_shape], [work, mid, pltpu.VMEM(shape, F32)], flag,
    )
    modes = solve(n, hat, coef, other)
    (pot,) = local_call(last_kernel, [modes, pot, table_xt, table_y], [shape], [mid])
    return (d[None], fx[None], fy[None], pot[None])


def solution(mesh):
    field = P(("grp", "tm"), None, None)
    flat = P("grp", None)
    return jax.shard_map(
        local,
        mesh=mesh,
        in_specs=(field, field, field, field, flat, flat),
        out_specs=(field, field, field, field),
        check_vma=False,
    )
```

```python
import functools

import jax
import jax.numpy as jnp
import ml_dtypes
import numpy as np
from jax import lax
from jax.experimental import pallas as pl
from jax.experimental.pallas import tpu as pltpu
from jax.sharding import PartitionSpec as P

NEWTON = 3

PRIMAL_STEP = 0.5
DUAL_STEP = 0.5
CONGESTION = 0.1
SCREENING = 0.05

CHUNKS = 4
TILE = 64
VMEM_BYTES = 26 * 1024 * 1024
F32 = jnp.float32
BF16 = jnp.bfloat16


def cosine_table(length):
    freq = np.arange(length, dtype=np.float64)[:, None]
    place = np.arange(length, dtype=np.float64)[None, :]
    scale = np.where(freq == 0, np.sqrt(1.0 / length), np.sqrt(2.0 / length))
    return scale * np.cos(np.pi * (place + 0.5) * freq / length)


def spectrum(length):
    return 2.0 - 2.0 * np.cos(np.pi * np.arange(length, dtype=np.float64) / length)


def halves(table):
    high = table.astype(np.float32).astype(ml_dtypes.bfloat16)
    low = (table - high.astype(np.float64)).astype(np.float32).astype(ml_dtypes.bfloat16)
    return np.stack([high, low])


def split(value):
    high = value.astype(BF16)
    return high, (value - high.astype(F32)).astype(BF16)


def product(a_high, a_low, b_high, b_low):
    dot = functools.partial(jnp.dot, preferred_element_type=F32)
    return dot(a_high, b_high) + (dot(a_low, b_high) + dot(a_high, b_low))


def inverse_of(value):
    rough = pl.reciprocal(value, approx=True)
    return rough * (2.0 - value * rough)


def two_sided(read, left, right, mid, write, rows):
    step = min(256, rows)
    for r0 in range(0, rows, step):
        high, low = split(read(r0, step))
        high, low = split(product(high, low, right[0], right[1]))
        mid[0, r0 : r0 + step, :] = high
        mid[1, r0 : r0 + step, :] = low
    for r0 in range(0, rows, step):
        here = slice(r0, r0 + step)
        write(r0, step, product(left[0, here, :], left[1, here, :], mid[0], mid[1]))


def proximal(density, flux_x, flux_y, time_grad, grad_x, grad_y, running_cost):
    moment_x = flux_x + PRIMAL_STEP * grad_x
    moment_y = flux_y + PRIMAL_STEP * grad_y
    kinetic = 0.5 * PRIMAL_STEP * (moment_x * moment_x + moment_y * moment_y)
    slope = 1.0 + CONGESTION * PRIMAL_STEP
    offset = density + PRIMAL_STEP * (time_grad - running_cost)
    root = jnp.exp2(jnp.log2(kinetic * (1.0 / slope)) * (1.0 / 3.0))
    guess = jnp.maximum(offset * (1.0 / slope), 0.0) + root
    for sweep in range(NEWTON):
        shifted = guess + PRIMAL_STEP
        linear = slope * guess - offset
        residue = linear * shifted * shifted - kinetic
        derivative = slope * shifted * shifted + 2.0 * linear * shifted
        guess = jnp.maximum(guess - residue * inverse_of(derivative), 0.0)
    weight = guess * inverse_of(guess + PRIMAL_STEP)
    return (guess, weight * moment_x, weight * moment_y)


def forward_half(flag, fields, pot, following, cost, init, table_x, table_yt, outs, hat, work, mid):
    density, flux_x, flux_y = fields
    rows, cols = pot.shape
    first = flag[0] == 1
    last = flag[1] == 1

    def tile(index, carry):
        r0 = pl.multiple_of(index * TILE, TILE)
        here = pl.ds(r0, TILE)
        row = lax.broadcasted_iota(jnp.int32, (TILE, cols), 0)
        col = lax.broadcasted_iota(jnp.int32, (TILE, cols), 1)
        p = pot[here, :]
        below = pl.multiple_of(jnp.minimum(r0 + TILE, rows - 8), 8)
        edge = pot[pl.ds(below, 8), :][0:1, :]
        p_down = jnp.where(row == TILE - 1, edge, pltpu.roll(p, TILE - 1, 0))
        grad_x = jnp.where(row + r0 == rows - 1, 0.0, p_down - p)
        grad_y = jnp.where(col == cols - 1, 0.0, pltpu.roll(p, cols - 1, 1) - p)
        time_grad = jnp.where(last, 0.0, following[here, :] - p)
        old, old_x, old_y = density[here, :], flux_x[here, :], flux_y[here, :]
        new, new_x, new_y = proximal(old, old_x, old_y, time_grad, grad_x, grad_y, cost[here, :])
        outs[0][here, :] = new
        outs[1][here, :] = new_x
        outs[2][here, :] = new_y
        bar = 2.0 * new - old
        bar_x = 2.0 * new_x - old_x
        bar_y = jnp.where(col == cols - 1, 0.0, 2.0 * new_y - old_y)
        div_y = bar_y - jnp.where(col == 0, 0.0, pltpu.roll(bar_y, 1, 1))
        bar_x = jnp.where(row + r0 == rows - 1, 0.0, bar_x)
        before = jnp.where(row == 0, carry, pltpu.roll(bar_x, 1, 0))
        start = jnp.where(first, init[here, :], 0.0)
        work[1, here, :] = bar
        work[0, here, :] = bar - start + div_y + (bar_x - before)
        return bar_x[TILE - 1 : TILE, :]

    lax.fori_loop(0, rows // TILE, tile, jnp.zeros((1, cols), F32))

    for part in range(2):
        def read(r0, step):
            return work[part, r0 : r0 + step, :]

        def write(r0, step, value):
            hat[part, r0 : r0 + step, :] = value

        two_sided(read, table_x, table_yt, mid, write, rows)


def backward_half(modes, part, pot, table_xt, table_y, out, mid):
    def read(r0, step):
        return modes[part, r0 : r0 + step, :]

    def write(r0, step, value):
        here = slice(r0, r0 + step)
        out[here, :] = pot[here, :] + DUAL_STEP * value

    two_sided(read, table_xt, table_y, mid, write, pot.shape[0])


def first_kernel(flag, density, flux_x, flux_y, pot, following, cost, init, tx, tyt, o_d, o_x, o_y, hat, work, mid):
    forward_half(flag, (density, flux_x, flux_y), pot, following, cost, init, tx, tyt, (o_d, o_x, o_y), hat, work, mid)


def middle_kernel(
    flag, modes, density, flux_x, flux_y, pot, following, cost, init, tx, txt, ty, tyt,
    o_d, o_x, o_y, o_p, hat, work, mid, moved,
):
    backward_half(modes, 0, pot, txt, ty, o_p, mid)
    backward_half(modes, 1, following, txt, ty, moved, mid)
    forward_half(flag, (density, flux_x, flux_y), o_p, moved, cost, init, tx, tyt, (o_d, o_x, o_y), hat, work, mid)


def last_kernel(modes, pot, txt, ty, o_p, mid):
    backward_half(modes, 0, pot, txt, ty, o_p, mid)


def solve_kernel(
    n, wd, coef, other, x, wd_in, ab_out, ab_in, ab_own, p_in, p_out, q_in, q_out, give, got, own, x_out,
    core_s, core_r, y_s, y_r, p_s, p_r, q_s, q_r, ret_s, ret_r, x_s, x_r,
):
    me = lax.axis_index("tm")
    core = lax.rem(me, 2)
    side = lax.rem(me // 2, 2)
    g = me // 4
    groups = n // 4
    mate = me + 1 - 2 * core
    across = me + 2 - 4 * side
    ahead, behind = me + 4, me - 4
    half = wd.shape[1] // 2
    quarter = half // 2
    rows = quarter // CHUNKS
    cols = wd.shape[2]

    barrier = pltpu.get_barrier_semaphore()
    pl.semaphore_signal(barrier, inc=1, device_id={"tm": mate}, device_id_type=pl.DeviceIdType.MESH)
    pl.semaphore_signal(barrier, inc=1, device_id={"tm": across}, device_id_type=pl.DeviceIdType.MESH)

    @pl.when(g > 0)
    def _():
        pl.semaphore_signal(barrier, inc=1, device_id={"tm": behind}, device_id_type=pl.DeviceIdType.MESH)

    @pl.when(g < groups - 1)
    def _():
        pl.semaphore_signal(barrier, inc=1, device_id={"tm": ahead}, device_id_type=pl.DeviceIdType.MESH)

    @pl.when(g == 0)
    def _():
        p_in[...] = jnp.zeros_like(p_in)

    @pl.when(g == groups - 1)
    def _():
        q_in[...] = jnp.zeros_like(q_in)

    peers = 2 + (g > 0).astype(jnp.int32) + (g < groups - 1).astype(jnp.int32)
    pl.semaphore_wait(barrier, peers)

    def remote(src, dst, send, recv, target):
        return pltpu.make_async_remote_copy(
            src_ref=src, dst_ref=dst, send_sem=send, recv_sem=recv,
            device_id={"tm": target}, device_id_type=pl.DeviceIdType.MESH,
        )

    def at(k):
        return pl.ds(pl.multiple_of(k * rows, rows), rows)

    def in_half(k):
        part = jnp.where(k < CHUNKS, 1 - side, side)
        return pl.multiple_of(part * quarter + lax.rem(k, CHUNKS) * rows, rows)

    def core_copy(k):
        src = wd.at[:, pl.ds(pl.multiple_of((1 - core) * half + in_half(k), rows), rows), :]
        return remote(src, wd_in.at[:, pl.ds(in_half(k), rows), :], core_s.at[k], core_r.at[k], mate)

    def y_copy(k):
        return remote(ab_out.at[:, at(k), :], ab_in.at[:, at(k), :], y_s.at[k], y_r.at[k], across)

    def p_copy(k):
        return remote(p_out.at[at(k), :], p_in.at[at(k), :], p_s.at[k], p_r.at[k], ahead)

    def q_copy(k):
        return remote(q_out.at[at(k), :], q_in.at[at(k), :], q_s.at[k], q_r.at[k], behind)

    def ret_copy(part, k):
        return remote(give.at[part, at(k), :], got.at[part, at(k), :], ret_s.at[part, k], ret_r.at[part, k], across)

    def x_copy(k):
        here = pl.ds(in_half(k), rows)
        there = pl.ds(pl.multiple_of(core * half + in_half(k), rows), rows)
        return remote(x_out.at[:, here, :], x.at[:, there, :], x_s.at[k], x_r.at[k], mate)

    def loop(count, body):
        lax.fori_loop(0, count, lambda k, c: (body(k), c)[1], 0)

    loop(2 * CHUNKS, lambda k: core_copy(k).start())

    low = core == 0

    def sources(k):
        here = pl.ds(in_half(k), rows)
        mine = pl.ds(pl.multiple_of(core * half + in_half(k), rows), rows)
        w_a, d_a = wd[0, mine, :], wd[1, mine, :]
        w_b, d_b = wd_in[0, here, :], wd_in[1, here, :]
        w0 = jnp.where(low, w_a, w_b)
        s1 = jnp.where(low, w_b - d_a, w_a - d_b)
        d1 = jnp.where(low, d_b, d_a)
        return w0, s1, d1, [coef[j, here, :] for j in range(6)]

    def carries(k):
        w0, s1, d1, (f0, f1, h0, h1, h2, _) = sources(k)
        return f1 * (s1 + f0 * w0) - d1, h0 * (w0 + h1 * (s1 - h2 * d1))

    def out_chunk(k):
        core_copy(k).wait_recv()
        a, b = carries(k)
        ab_out[0, at(k), :] = a
        ab_out[1, at(k), :] = b
        y_copy(k).start()

    loop(CHUNKS, out_chunk)

    def own_chunk(k):
        core_copy(k + CHUNKS).wait_recv()
        a, b = carries(k + CHUNKS)
        ab_own[0, at(k), :] = a
        ab_own[1, at(k), :] = b

    loop(CHUNKS, own_chunk)

    left = side == 0

    def ordered(part, k, first, second):
        here = pl.ds(in_half(k + CHUNKS), rows)
        mine, theirs = ab_own[part, at(k), :], ab_in[part, at(k), :]
        rate, rate_other = coef[first, here, :] * coef[second, here, :], other[part, at(k), :]
        return (
            jnp.where(left, mine, theirs), jnp.where(left, rate, rate_other),
            jnp.where(left, theirs, mine), jnp.where(left, rate_other, rate),
        )

    def step(s):
        @pl.when(s < CHUNKS)
        def _():
            y_copy(s).wait_recv()

        kp = s - g

        @pl.when((kp >= 0) & (kp < CHUNKS))
        def _():
            @pl.when(g > 0)
            def _():
                p_copy(kp).wait_recv()

            a0, r0, a1, r1 = ordered(0, kp, 0, 1)
            enter = p_in[at(kp), :]
            middle = a0 + r0 * enter

            @pl.when(g < groups - 1)
            def _():
                p_out[at(kp), :] = a1 + r1 * middle
                p_copy(kp).start()

            own[0, at(kp), :] = jnp.where(left, enter, middle)
            give[0, at(kp), :] = jnp.where(left, middle, enter)
            ret_copy(0, kp).start()

        kq = s - (groups - 1 - g)

        @pl.when((kq >= 0) & (kq < CHUNKS))
        def _():
            @pl.when(g < groups - 1)
            def _():
                q_copy(kq).wait_recv()

            b0, r0, b1, r1 = ordered(1, kq, 2, 3)
            enter = q_in[at(kq), :]
            middle = b1 + r1 * enter

            @pl.when(g > 0)
            def _():
                q_out[at(kq), :] = b0 + r0 * middle
                q_copy(kq).start()

            own[1, at(kq), :] = jnp.where(left, middle, enter)
            give[1, at(kq), :] = jnp.where(left, enter, middle)
            ret_copy(1, kq).start()

    loop(CHUNKS + groups - 1, step)

    def finish(k, carry_p, carry_q):
        w0, s1, d1, (f0, f1, h0, h1, h2, g0) = sources(k)
        q2 = carry_q - h2 * d1
        q1 = h1 * (s1 + q2)
        x0 = (w0 + carry_p + q1) * g0
        x1 = h1 * x0 + q1
        x2 = h2 * x1 + q2
        here = pl.ds(in_half(k), rows)
        mine = pl.ds(pl.multiple_of(core * half + in_half(k), rows), rows)
        x[0, mine, :] = jnp.where(low, x0, x1)
        x[1, mine, :] = jnp.where(low, x1, x2)
        x_out[0, here, :] = jnp.where(low, x1, x0)
        x_out[1, here, :] = jnp.where(low, x2, x1)
        x_copy(k).start()

    loop(CHUNKS, lambda k: finish(k + CHUNKS, own[0, at(k), :], own[1, at(k), :]))

    def returned(k):
        ret_copy(0, k).wait_recv()
        ret_copy(1, k).wait_recv()
        finish(k, got[0, at(k), :], got[1, at(k), :])

    loop(CHUNKS, returned)

    def drain(k):
        core_copy(k).wait_send()
        x_copy(k).wait_send()
        x_copy(k).wait_recv()

    loop(2 * CHUNKS, drain)

    def drain_more(k):
        y_copy(k).wait_send()
        ret_copy(0, k).wait_send()
        ret_copy(1, k).wait_send()

        @pl.when(g < groups - 1)
        def _():
            p_copy(k).wait_send()

        @pl.when(g > 0)
        def _():
            q_copy(k).wait_send()

    loop(CHUNKS, drain_more)


def vmem(count):
    return [pl.BlockSpec(memory_space=pltpu.VMEM)] * count


def local_call(kernel, inputs, outs, scratch, flag=None):
    specs = vmem(len(inputs))
    if flag is not None:
        specs = [pl.BlockSpec(memory_space=pltpu.SMEM)] + specs
        inputs = [flag] + inputs
    return pl.pallas_call(
        kernel,
        out_shape=[jax.ShapeDtypeStruct(shape, F32) for shape in outs],
        in_specs=specs,
        out_specs=vmem(len(outs)),
        scratch_shapes=scratch,
        compiler_params=pltpu.CompilerParams(vmem_limit_bytes=VMEM_BYTES),
    )(*inputs)


def solve(n, wd, coef, other):
    _, rows, cols = wd.shape
    half, quarter = rows // 2, rows // 4
    dma = pltpu.SemaphoreType.DMA
    two = pltpu.VMEM((2, quarter, cols), F32)
    one = pltpu.VMEM((quarter, cols), F32)
    return pl.pallas_call(
        functools.partial(solve_kernel, n),
        out_shape=jax.ShapeDtypeStruct((2, rows, cols), F32),
        in_specs=vmem(3),
        out_specs=pl.BlockSpec(memory_space=pltpu.VMEM),
        scratch_shapes=[
            pltpu.VMEM((2, half, cols), F32), two, two, two, one, one, one, one, two, two, two,
            pltpu.VMEM((2, half, cols), F32),
            dma((2 * CHUNKS,)), dma((2 * CHUNKS,)), dma((CHUNKS,)), dma((CHUNKS,)),
            dma((CHUNKS,)), dma((CHUNKS,)), dma((CHUNKS,)), dma((CHUNKS,)),
            dma((2, CHUNKS)), dma((2, CHUNKS)), dma((2 * CHUNKS,)), dma((2 * CHUNKS,)),
        ],
        compiler_params=pltpu.CompilerParams(
            vmem_limit_bytes=VMEM_BYTES, collective_id=0, has_side_effects=True
        ),
    )(wd, coef, other)


def time_factors(n, position, rows, cols):
    lam_x = jnp.asarray(spectrum(rows), F32)
    lam_y = jnp.asarray(spectrum(cols), F32)
    half, quarter = rows // 2, rows // 4
    core, side, chip = position % 2, (position // 2) % 2, position // 2

    def pivots(start, count):
        mu = SCREENING + lax.dynamic_slice_in_dim(lam_x, start, count)[:, None] + lam_y[None, :]
        r = 2.0 / (mu + 2.0 + jnp.sqrt(mu * (mu + 4.0)))
        log_r = jnp.log(r)

        def inverse(i):
            power = jnp.exp(log_r * (2 * i + 1).astype(F32))
            return r * (1.0 + power) / (1.0 + power * r * r)

        return mu, inverse

    mu, inverse = pivots(core * half, half)
    i0 = 2 * chip
    h1 = inverse(n - 2 - i0)
    h2 = jnp.where(i0 + 2 == n, 0.0, inverse(jnp.maximum(n - 3 - i0, 0)))
    g0 = 1.0 / (mu + 2.0 - inverse(i0 - 1) - h1)
    coef = jnp.stack([inverse(i0), inverse(i0 + 1), inverse(n - 1 - i0), h1, h2, g0])
    _, inverse = pivots(core * half + side * quarter, quarter)
    j0 = 2 * (chip + 1 - 2 * side)
    other = jnp.stack([inverse(j0) * inverse(j0 + 1), inverse(n - 1 - j0) * inverse(n - 2 - j0)])
    return coef, other


def local(density, flux_x, flux_y, potential, initial_density, running_cost):
    n = lax.axis_size("tm")
    position = lax.axis_index("tm")
    _, rows, cols = density.shape
    shape = (rows, cols)
    following = lax.ppermute(potential[0], "tm", [(t, t - 1) for t in range(1, n)])
    coef, other = time_factors(n, position, rows, cols)
    flag = jnp.stack([position == 0, position == n - 1]).astype(jnp.int32)
    tx, ty = cosine_table(rows), cosine_table(cols)
    table_x, table_xt = jnp.asarray(halves(tx)), jnp.asarray(halves(tx.T))
    table_y, table_yt = jnp.asarray(halves(ty)), jnp.asarray(halves(ty.T))
    work = pltpu.VMEM((2, rows, cols), F32)
    mid = pltpu.VMEM((2, rows, cols), BF16)
    three = [shape] * 3
    hat_shape = (2, rows, cols)

    d, fx, fy, hat = local_call(
        first_kernel,
        [density[0], flux_x[0], flux_y[0], potential[0], following, running_cost, initial_density, table_x, table_yt],
        three + [hat_shape], [work, mid], flag,
    )
    modes = solve(n, hat, coef, other)
    d, fx, fy, pot, hat = local_call(
        middle_kernel,
        [modes, d, fx, fy, potential[0], following, running_cost, initial_density, table_x, table_xt, table_y, table_yt],
        three + [shape, hat_shape], [work, mid, pltpu.VMEM(shape, F32)], flag,
    )
    modes = solve(n, hat, coef, other)
    (pot,) = local_call(last_kernel, [modes, pot, table_xt, table_y], [shape], [mid])
    return (d[None], fx[None], fy[None], pot[None])


def solution(mesh):
    field = P(("grp", "tm"), None, None)
    flat = P("grp", None)
    return jax.shard_map(
        local,
        mesh=mesh,
        in_specs=(field, field, field, field, flat, flat),
        out_specs=(field, field, field, field),
        check_vma=False,
    )
```

```python
import functools

import jax
import jax.numpy as jnp
import ml_dtypes
import numpy as np
from jax import lax
from jax.experimental import pallas as pl
from jax.experimental.pallas import tpu as pltpu
from jax.sharding import PartitionSpec as P

NEWTON = 3

PRIMAL_STEP = 0.5
DUAL_STEP = 0.5
CONGESTION = 0.1
SCREENING = 0.05

CHUNKS = 4
TILE = 64
VMEM_BYTES = 26 * 1024 * 1024
F32 = jnp.float32
BF16 = jnp.bfloat16


def cosine_table(length):
    freq = np.arange(length, dtype=np.float64)[:, None]
    place = np.arange(length, dtype=np.float64)[None, :]
    scale = np.where(freq == 0, np.sqrt(1.0 / length), np.sqrt(2.0 / length))
    return scale * np.cos(np.pi * (place + 0.5) * freq / length)


def spectrum(length):
    return 2.0 - 2.0 * np.cos(np.pi * np.arange(length, dtype=np.float64) / length)


def halves(table):
    high = table.astype(np.float32).astype(ml_dtypes.bfloat16)
    low = (table - high.astype(np.float64)).astype(np.float32).astype(ml_dtypes.bfloat16)
    return np.stack([high, low])


def split(value):
    high = value.astype(BF16)
    return high, (value - high.astype(F32)).astype(BF16)


def product(a_high, a_low, b_high, b_low):
    dot = functools.partial(jnp.dot, preferred_element_type=F32)
    return dot(a_high, b_high) + (dot(a_low, b_high) + dot(a_high, b_low))


def inverse_of(value):
    rough = pl.reciprocal(value, approx=True)
    return rough * (2.0 - value * rough)


def two_sided(read, left, right, mid, write, rows):
    step = min(256, rows)
    for r0 in range(0, rows, step):
        high, low = split(read(r0, step))
        high, low = split(product(high, low, right[0], right[1]))
        mid[0, r0 : r0 + step, :] = high
        mid[1, r0 : r0 + step, :] = low
    for r0 in range(0, rows, step):
        here = slice(r0, r0 + step)
        write(r0, step, product(left[0, here, :], left[1, here, :], mid[0], mid[1]))


def proximal(density, flux_x, flux_y, time_grad, grad_x, grad_y, running_cost):
    moment_x = flux_x + PRIMAL_STEP * grad_x
    moment_y = flux_y + PRIMAL_STEP * grad_y
    kinetic = 0.5 * PRIMAL_STEP * (moment_x * moment_x + moment_y * moment_y)
    slope = 1.0 + CONGESTION * PRIMAL_STEP
    offset = density + PRIMAL_STEP * (time_grad - running_cost)
    root = jnp.exp2(jnp.log2(kinetic * (1.0 / slope)) * (1.0 / 3.0))
    guess = jnp.maximum(offset * (1.0 / slope), 0.0) + root
    for sweep in range(NEWTON):
        shifted = guess + PRIMAL_STEP
        linear = slope * guess - offset
        residue = linear * shifted * shifted - kinetic
        derivative = slope * shifted * shifted + 2.0 * linear * shifted
        guess = jnp.maximum(guess - residue * inverse_of(derivative), 0.0)
    weight = guess * inverse_of(guess + PRIMAL_STEP)
    return (guess, weight * moment_x, weight * moment_y)


def forward_half(first, last, fields, pot, following, cost, init, table_x, table_yt, outs, hat, work, mid, ready=None):
    density, flux_x, flux_y = fields
    rows, cols = pot.shape

    def tile(index, carry):
        if ready is not None:
            ready(index)
        r0 = pl.multiple_of(index * TILE, TILE)
        here = pl.ds(r0, TILE)
        row = lax.broadcasted_iota(jnp.int32, (TILE, cols), 0)
        col = lax.broadcasted_iota(jnp.int32, (TILE, cols), 1)
        p = pot[here, :]
        below = pl.multiple_of(jnp.minimum(r0 + TILE, rows - 8), 8)
        edge = pot[pl.ds(below, 8), :][0:1, :]
        p_down = jnp.where(row == TILE - 1, edge, pltpu.roll(p, TILE - 1, 0))
        grad_x = jnp.where(row + r0 == rows - 1, 0.0, p_down - p)
        grad_y = jnp.where(col == cols - 1, 0.0, pltpu.roll(p, cols - 1, 1) - p)
        time_grad = jnp.where(last, 0.0, following[here, :] - p)
        old, old_x, old_y = density[here, :], flux_x[here, :], flux_y[here, :]
        new, new_x, new_y = proximal(old, old_x, old_y, time_grad, grad_x, grad_y, cost[here, :])
        outs[0][here, :] = new
        outs[1][here, :] = new_x
        outs[2][here, :] = new_y
        bar = 2.0 * new - old
        bar_x = 2.0 * new_x - old_x
        bar_y = jnp.where(col == cols - 1, 0.0, 2.0 * new_y - old_y)
        div_y = bar_y - jnp.where(col == 0, 0.0, pltpu.roll(bar_y, 1, 1))
        bar_x = jnp.where(row + r0 == rows - 1, 0.0, bar_x)
        before = jnp.where(row == 0, carry, pltpu.roll(bar_x, 1, 0))
        start = jnp.where(first, init[here, :], 0.0)
        work[1, here, :] = bar
        work[0, here, :] = bar - start + div_y + (bar_x - before)
        return bar_x[TILE - 1 : TILE, :]

    lax.fori_loop(0, rows // TILE, tile, jnp.zeros((1, cols), F32))

    for part in range(2):
        def read(r0, step):
            return work[part, r0 : r0 + step, :]

        def write(r0, step, value):
            hat[part, r0 : r0 + step, :] = value

        two_sided(read, table_x, table_yt, mid, write, rows)


def backward_half(modes, part, pot, table_xt, table_y, out, mid):
    def read(r0, step):
        return modes[part, r0 : r0 + step, :]

    def write(r0, step, value):
        here = slice(r0, r0 + step)
        out[here, :] = pot[here, :] + DUAL_STEP * value

    two_sided(read, table_xt, table_y, mid, write, pot.shape[0])


def factors(n, me, mu_ref, coef, other):
    half, cols = coef.shape[1:]
    quarter = half // 2
    core, side, chip = lax.rem(me, 2), lax.rem(me // 2, 2), me // 2
    ends = chip == n // 2 - 1

    def roots(row):
        mu = mu_ref[pl.ds(pl.multiple_of(row, TILE), TILE), :]
        r = 2.0 / (mu + 2.0 + jnp.sqrt(mu * (mu + 4.0)))
        return mu, r, r * r, jnp.log(r)

    def three(i, r, r2, log_r):
        power = jnp.exp(log_r * (2 * i + 1).astype(F32))
        terms = []
        for _ in range(4):
            terms.append(1.0 + power)
            power = power * r2
        return [r * terms[j] / terms[j + 1] for j in range(3)]

    def main(k, c):
        mu, r, r2, log_r = roots(core * half + k * TILE)
        here = pl.ds(pl.multiple_of(k * TILE, TILE), TILE)
        before, f0, f1 = three(2 * chip - 1, r, r2, log_r)
        h2, h1, h0 = three(n - 3 - 2 * chip, r, r2, log_r)
        g0 = 1.0 / (mu + 2.0 - before - h1)
        for j, value in enumerate((f0, f1, h0, h1, jnp.where(ends, 0.0, h2), g0)):
            coef[j, here, :] = value
        return c

    lax.fori_loop(0, half // TILE, main, 0)

    def rest(k, c):
        _, r, r2, log_r = roots(core * half + side * quarter + k * TILE)
        here = pl.ds(pl.multiple_of(k * TILE, TILE), TILE)
        j0 = 2 * (chip + 1 - 2 * side)
        for part, i in enumerate((j0, n - 2 - j0)):
            one, two, _ = three(i, r, r2, log_r)
            other[part, here, :] = one * two
        return c

    lax.fori_loop(0, quarter // TILE, rest, 0)


def first_kernel(
    n, density, flux_x, flux_y, pot, cost, init, tx, tyt, mu,
    o_d, o_x, o_y, hat, following, coef, other, work, mid, send, recv,
):
    me = lax.axis_index("tm")
    chunks = pot.shape[0] // TILE
    barrier = pltpu.get_barrier_semaphore()

    @pl.when(me > 0)
    def _():
        pl.semaphore_signal(barrier, inc=1, device_id={"tm": me - 1}, device_id_type=pl.DeviceIdType.MESH)

    @pl.when(me < n - 1)
    def _():
        pl.semaphore_signal(barrier, inc=1, device_id={"tm": me + 1}, device_id_type=pl.DeviceIdType.MESH)

    @pl.when(me == n - 1)
    def _():
        following[...] = jnp.zeros_like(following)

    pl.semaphore_wait(barrier, (me > 0).astype(jnp.int32) + (me < n - 1).astype(jnp.int32))

    def copy(k):
        here = pl.ds(pl.multiple_of(k * TILE, TILE), TILE)
        return pltpu.make_async_remote_copy(
            src_ref=pot.at[here, :], dst_ref=following.at[here, :], send_sem=send.at[k], recv_sem=recv.at[k],
            device_id={"tm": me - 1}, device_id_type=pl.DeviceIdType.MESH,
        )

    @pl.when(me > 0)
    def _():
        lax.fori_loop(0, chunks, lambda k, c: (copy(k).start(), c)[1], 0)

    factors(n, me, mu, coef, other)

    def ready(k):
        @pl.when(me < n - 1)
        def _():
            copy(k).wait_recv()

    forward_half(
        me == 0, me == n - 1, (density, flux_x, flux_y), pot, following, cost, init, tx, tyt,
        (o_d, o_x, o_y), hat, work, mid, ready,
    )

    @pl.when(me > 0)
    def _():
        lax.fori_loop(0, chunks, lambda k, c: (copy(k).wait_send(), c)[1], 0)


def middle_kernel(
    flag, modes, density, flux_x, flux_y, pot, following, cost, init, tx, txt, ty, tyt,
    o_d, o_x, o_y, o_p, hat, work, mid, moved,
):
    backward_half(modes, 0, pot, txt, ty, o_p, mid)
    backward_half(modes, 1, following, txt, ty, moved, mid)
    first, last = flag[0] == 1, flag[1] == 1
    forward_half(first, last, (density, flux_x, flux_y), o_p, moved, cost, init, tx, tyt, (o_d, o_x, o_y), hat, work, mid)


def last_kernel(modes, pot, txt, ty, o_p, mid):
    backward_half(modes, 0, pot, txt, ty, o_p, mid)


def solve_kernel(
    n, wd, coef, other, x, wd_in, ab_out, ab_in, ab_own, p_in, p_out, q_in, q_out, give, got, own, x_out,
    core_s, core_r, y_s, y_r, p_s, p_r, q_s, q_r, ret_s, ret_r, x_s, x_r,
):
    me = lax.axis_index("tm")
    core = lax.rem(me, 2)
    side = lax.rem(me // 2, 2)
    g = me // 4
    groups = n // 4
    mate = me + 1 - 2 * core
    across = me + 2 - 4 * side
    ahead, behind = me + 4, me - 4
    half = wd.shape[1] // 2
    quarter = half // 2
    rows = quarter // CHUNKS
    cols = wd.shape[2]

    barrier = pltpu.get_barrier_semaphore()
    pl.semaphore_signal(barrier, inc=1, device_id={"tm": mate}, device_id_type=pl.DeviceIdType.MESH)
    pl.semaphore_signal(barrier, inc=1, device_id={"tm": across}, device_id_type=pl.DeviceIdType.MESH)

    @pl.when(g > 0)
    def _():
        pl.semaphore_signal(barrier, inc=1, device_id={"tm": behind}, device_id_type=pl.DeviceIdType.MESH)

    @pl.when(g < groups - 1)
    def _():
        pl.semaphore_signal(barrier, inc=1, device_id={"tm": ahead}, device_id_type=pl.DeviceIdType.MESH)

    @pl.when(g == 0)
    def _():
        p_in[...] = jnp.zeros_like(p_in)

    @pl.when(g == groups - 1)
    def _():
        q_in[...] = jnp.zeros_like(q_in)

    peers = 2 + (g > 0).astype(jnp.int32) + (g < groups - 1).astype(jnp.int32)
    pl.semaphore_wait(barrier, peers)

    def remote(src, dst, send, recv, target):
        return pltpu.make_async_remote_copy(
            src_ref=src, dst_ref=dst, send_sem=send, recv_sem=recv,
            device_id={"tm": target}, device_id_type=pl.DeviceIdType.MESH,
        )

    def at(k):
        return pl.ds(pl.multiple_of(k * rows, rows), rows)

    def in_half(k):
        part = jnp.where(k < CHUNKS, 1 - side, side)
        return pl.multiple_of(part * quarter + lax.rem(k, CHUNKS) * rows, rows)

    def core_copy(k):
        src = wd.at[:, pl.ds(pl.multiple_of((1 - core) * half + in_half(k), rows), rows), :]
        return remote(src, wd_in.at[:, pl.ds(in_half(k), rows), :], core_s.at[k], core_r.at[k], mate)

    def y_copy(k):
        return remote(ab_out.at[:, at(k), :], ab_in.at[:, at(k), :], y_s.at[k], y_r.at[k], across)

    def p_copy(k):
        return remote(p_out.at[at(k), :], p_in.at[at(k), :], p_s.at[k], p_r.at[k], ahead)

    def q_copy(k):
        return remote(q_out.at[at(k), :], q_in.at[at(k), :], q_s.at[k], q_r.at[k], behind)

    def ret_copy(part, k):
        return remote(give.at[part, at(k), :], got.at[part, at(k), :], ret_s.at[part, k], ret_r.at[part, k], across)

    def x_copy(k):
        here = pl.ds(in_half(k), rows)
        there = pl.ds(pl.multiple_of(core * half + in_half(k), rows), rows)
        return remote(x_out.at[:, here, :], x.at[:, there, :], x_s.at[k], x_r.at[k], mate)

    def loop(count, body):
        lax.fori_loop(0, count, lambda k, c: (body(k), c)[1], 0)

    loop(2 * CHUNKS, lambda k: core_copy(k).start())

    low = core == 0

    def sources(k):
        here = pl.ds(in_half(k), rows)
        mine = pl.ds(pl.multiple_of(core * half + in_half(k), rows), rows)
        w_a, d_a = wd[0, mine, :], wd[1, mine, :]
        w_b, d_b = wd_in[0, here, :], wd_in[1, here, :]
        w0 = jnp.where(low, w_a, w_b)
        s1 = jnp.where(low, w_b - d_a, w_a - d_b)
        d1 = jnp.where(low, d_b, d_a)
        return w0, s1, d1, [coef[j, here, :] for j in range(6)]

    def carries(k):
        w0, s1, d1, (f0, f1, h0, h1, h2, _) = sources(k)
        return f1 * (s1 + f0 * w0) - d1, h0 * (w0 + h1 * (s1 - h2 * d1))

    def out_chunk(k):
        core_copy(k).wait_recv()
        a, b = carries(k)
        ab_out[0, at(k), :] = a
        ab_out[1, at(k), :] = b
        y_copy(k).start()

    loop(CHUNKS, out_chunk)

    def own_chunk(k):
        core_copy(k + CHUNKS).wait_recv()
        a, b = carries(k + CHUNKS)
        ab_own[0, at(k), :] = a
        ab_own[1, at(k), :] = b

    loop(CHUNKS, own_chunk)

    left = side == 0

    def ordered(part, k, first, second):
        here = pl.ds(in_half(k + CHUNKS), rows)
        mine, theirs = ab_own[part, at(k), :], ab_in[part, at(k), :]
        rate, rate_other = coef[first, here, :] * coef[second, here, :], other[part, at(k), :]
        return (
            jnp.where(left, mine, theirs), jnp.where(left, rate, rate_other),
            jnp.where(left, theirs, mine), jnp.where(left, rate_other, rate),
        )

    def step(s):
        @pl.when(s < CHUNKS)
        def _():
            y_copy(s).wait_recv()

        kp = s - g

        @pl.when((kp >= 0) & (kp < CHUNKS))
        def _():
            @pl.when(g > 0)
            def _():
                p_copy(kp).wait_recv()

            a0, r0, a1, r1 = ordered(0, kp, 0, 1)
            enter = p_in[at(kp), :]
            middle = a0 + r0 * enter

            @pl.when(g < groups - 1)
            def _():
                p_out[at(kp), :] = a1 + r1 * middle
                p_copy(kp).start()

            own[0, at(kp), :] = jnp.where(left, enter, middle)
            give[0, at(kp), :] = jnp.where(left, middle, enter)
            ret_copy(0, kp).start()

        kq = s - (groups - 1 - g)

        @pl.when((kq >= 0) & (kq < CHUNKS))
        def _():
            @pl.when(g < groups - 1)
            def _():
                q_copy(kq).wait_recv()

            b0, r0, b1, r1 = ordered(1, kq, 2, 3)
            enter = q_in[at(kq), :]
            middle = b1 + r1 * enter

            @pl.when(g > 0)
            def _():
                q_out[at(kq), :] = b0 + r0 * middle
                q_copy(kq).start()

            own[1, at(kq), :] = jnp.where(left, middle, enter)
            give[1, at(kq), :] = jnp.where(left, enter, middle)
            ret_copy(1, kq).start()

    loop(CHUNKS + groups - 1, step)

    def finish(k, carry_p, carry_q):
        w0, s1, d1, (f0, f1, h0, h1, h2, g0) = sources(k)
        q2 = carry_q - h2 * d1
        q1 = h1 * (s1 + q2)
        x0 = (w0 + carry_p + q1) * g0
        x1 = h1 * x0 + q1
        x2 = h2 * x1 + q2
        here = pl.ds(in_half(k), rows)
        mine = pl.ds(pl.multiple_of(core * half + in_half(k), rows), rows)
        x[0, mine, :] = jnp.where(low, x0, x1)
        x[1, mine, :] = jnp.where(low, x1, x2)
        x_out[0, here, :] = jnp.where(low, x1, x0)
        x_out[1, here, :] = jnp.where(low, x2, x1)
        x_copy(k).start()

    loop(CHUNKS, lambda k: finish(k + CHUNKS, own[0, at(k), :], own[1, at(k), :]))

    def returned(k):
        ret_copy(0, k).wait_recv()
        ret_copy(1, k).wait_recv()
        finish(k, got[0, at(k), :], got[1, at(k), :])

    loop(CHUNKS, returned)

    def drain(k):
        core_copy(k).wait_send()
        x_copy(k).wait_send()
        x_copy(k).wait_recv()

    loop(2 * CHUNKS, drain)

    def drain_more(k):
        y_copy(k).wait_send()
        ret_copy(0, k).wait_send()
        ret_copy(1, k).wait_send()

        @pl.when(g < groups - 1)
        def _():
            p_copy(k).wait_send()

        @pl.when(g > 0)
        def _():
            q_copy(k).wait_send()

    loop(CHUNKS, drain_more)


def vmem(count):
    return [pl.BlockSpec(memory_space=pltpu.VMEM)] * count


def local_call(kernel, inputs, outs, scratch, flag=None, collective=None):
    specs = vmem(len(inputs))
    if flag is not None:
        specs = [pl.BlockSpec(memory_space=pltpu.SMEM)] + specs
        inputs = [flag] + inputs
    params = dict(vmem_limit_bytes=VMEM_BYTES)
    if collective is not None:
        params.update(collective_id=collective, has_side_effects=True)
    return pl.pallas_call(
        kernel,
        out_shape=[jax.ShapeDtypeStruct(shape, F32) for shape in outs],
        in_specs=specs,
        out_specs=vmem(len(outs)),
        scratch_shapes=scratch,
        compiler_params=pltpu.CompilerParams(**params),
    )(*inputs)


def solve(n, wd, coef, other):
    _, rows, cols = wd.shape
    half, quarter = rows // 2, rows // 4
    dma = pltpu.SemaphoreType.DMA
    two = pltpu.VMEM((2, quarter, cols), F32)
    one = pltpu.VMEM((quarter, cols), F32)
    return pl.pallas_call(
        functools.partial(solve_kernel, n),
        out_shape=jax.ShapeDtypeStruct((2, rows, cols), F32),
        in_specs=vmem(3),
        out_specs=pl.BlockSpec(memory_space=pltpu.VMEM),
        scratch_shapes=[
            pltpu.VMEM((2, half, cols), F32), two, two, two, one, one, one, one, two, two, two,
            pltpu.VMEM((2, half, cols), F32),
            dma((2 * CHUNKS,)), dma((2 * CHUNKS,)), dma((CHUNKS,)), dma((CHUNKS,)),
            dma((CHUNKS,)), dma((CHUNKS,)), dma((CHUNKS,)), dma((CHUNKS,)),
            dma((2, CHUNKS)), dma((2, CHUNKS)), dma((2 * CHUNKS,)), dma((2 * CHUNKS,)),
        ],
        compiler_params=pltpu.CompilerParams(
            vmem_limit_bytes=VMEM_BYTES, collective_id=0, has_side_effects=True
        ),
    )(wd, coef, other)


def local(density, flux_x, flux_y, potential, initial_density, running_cost):
    n = lax.axis_size("tm")
    position = lax.axis_index("tm")
    _, rows, cols = density.shape
    shape = (rows, cols)
    mu = jnp.asarray(SCREENING + spectrum(rows)[:, None] + spectrum(cols)[None, :], F32)
    dma = pltpu.SemaphoreType.DMA((rows // TILE,))
    flag = jnp.stack([position == 0, position == n - 1]).astype(jnp.int32)
    tx, ty = cosine_table(rows), cosine_table(cols)
    table_x, table_xt = jnp.asarray(halves(tx)), jnp.asarray(halves(tx.T))
    table_y, table_yt = jnp.asarray(halves(ty)), jnp.asarray(halves(ty.T))
    work = pltpu.VMEM((2, rows, cols), F32)
    mid = pltpu.VMEM((2, rows, cols), BF16)
    three = [shape] * 3
    hat_shape = (2, rows, cols)

    d, fx, fy, hat, following, coef, other = local_call(
        functools.partial(first_kernel, n),
        [density[0], flux_x[0], flux_y[0], potential[0], running_cost, initial_density, table_x, table_yt, mu],
        three + [hat_shape, shape, (6, rows // 2, cols), (2, rows // 4, cols)],
        [work, mid, dma, dma], collective=1,
    )
    modes = solve(n, hat, coef, other)
    d, fx, fy, pot, hat = local_call(
        middle_kernel,
        [modes, d, fx, fy, potential[0], following, running_cost, initial_density, table_x, table_xt, table_y, table_yt],
        three + [shape, hat_shape], [work, mid, pltpu.VMEM(shape, F32)], flag,
    )
    modes = solve(n, hat, coef, other)
    (pot,) = local_call(last_kernel, [modes, pot, table_xt, table_y], [shape], [mid])
    return (d[None], fx[None], fy[None], pot[None])


def solution(mesh):
    field = P(("grp", "tm"), None, None)
    flat = P("grp", None)
    return jax.shard_map(
        local,
        mesh=mesh,
        in_specs=(field, field, field, field, flat, flat),
        out_specs=(field, field, field, field),
        check_vma=False,
    )
```

```python
import functools

import jax
import jax.numpy as jnp
import ml_dtypes
import numpy as np
from jax import lax
from jax.experimental import pallas as pl
from jax.experimental.pallas import tpu as pltpu
from jax.sharding import PartitionSpec as P

NEWTON = 3

PRIMAL_STEP = 0.5
DUAL_STEP = 0.5
CONGESTION = 0.1
SCREENING = 0.05

CHUNKS = 4
TILE = 64
VMEM_BYTES = 26 * 1024 * 1024
F32 = jnp.float32
BF16 = jnp.bfloat16


def cosine_table(length):
    freq = np.arange(length, dtype=np.float64)[:, None]
    place = np.arange(length, dtype=np.float64)[None, :]
    scale = np.where(freq == 0, np.sqrt(1.0 / length), np.sqrt(2.0 / length))
    return scale * np.cos(np.pi * (place + 0.5) * freq / length)


def spectrum(length):
    return 2.0 - 2.0 * np.cos(np.pi * np.arange(length, dtype=np.float64) / length)


def halves(table):
    high = table.astype(np.float32).astype(ml_dtypes.bfloat16)
    low = (table - high.astype(np.float64)).astype(np.float32).astype(ml_dtypes.bfloat16)
    return np.stack([high, low])


def split(value):
    high = value.astype(BF16)
    return high, (value - high.astype(F32)).astype(BF16)


def product(a_high, a_low, b_high, b_low):
    dot = functools.partial(jnp.dot, preferred_element_type=F32)
    return dot(a_high, b_high) + (dot(a_low, b_high) + dot(a_high, b_low))


def inverse_of(value):
    rough = pl.reciprocal(value, approx=True)
    return rough * (2.0 - value * rough)


def two_sided(read, left, right, mid, write, rows):
    step = min(256, rows)
    for r0 in range(0, rows, step):
        high, low = split(read(r0, step))
        high, low = split(product(high, low, right[0], right[1]))
        mid[0, r0 : r0 + step, :] = high
        mid[1, r0 : r0 + step, :] = low
    for r0 in range(0, rows, step):
        here = slice(r0, r0 + step)
        write(r0, step, product(left[0, here, :], left[1, here, :], mid[0], mid[1]))


def proximal(density, flux_x, flux_y, time_grad, grad_x, grad_y, running_cost):
    moment_x = flux_x + PRIMAL_STEP * grad_x
    moment_y = flux_y + PRIMAL_STEP * grad_y
    kinetic = 0.5 * PRIMAL_STEP * (moment_x * moment_x + moment_y * moment_y)
    slope = 1.0 + CONGESTION * PRIMAL_STEP
    offset = density + PRIMAL_STEP * (time_grad - running_cost)
    root = jnp.exp2(jnp.log2(kinetic * (1.0 / slope)) * (1.0 / 3.0))
    guess = jnp.maximum(offset * (1.0 / slope), 0.0) + root
    for sweep in range(NEWTON):
        shifted = guess + PRIMAL_STEP
        linear = slope * guess - offset
        residue = linear * shifted * shifted - kinetic
        derivative = slope * shifted * shifted + 2.0 * linear * shifted
        guess = jnp.maximum(guess - residue * inverse_of(derivative), 0.0)
    weight = guess * inverse_of(guess + PRIMAL_STEP)
    return (guess, weight * moment_x, weight * moment_y)


def forward_half(first, last, fields, pot, following, cost, init, table_x, table_yt, outs, hat, work, mid, ready=None):
    density, flux_x, flux_y = fields
    rows, cols = pot.shape

    def tile(index, carry):
        if ready is not None:
            ready(index)
        r0 = pl.multiple_of(index * TILE, TILE)
        here = pl.ds(r0, TILE)
        row = lax.broadcasted_iota(jnp.int32, (TILE, cols), 0)
        col = lax.broadcasted_iota(jnp.int32, (TILE, cols), 1)
        p = pot[here, :]
        below = pl.multiple_of(jnp.minimum(r0 + TILE, rows - 8), 8)
        edge = pot[pl.ds(below, 8), :][0:1, :]
        p_down = jnp.where(row == TILE - 1, edge, pltpu.roll(p, TILE - 1, 0))
        grad_x = jnp.where(row + r0 == rows - 1, 0.0, p_down - p)
        grad_y = jnp.where(col == cols - 1, 0.0, pltpu.roll(p, cols - 1, 1) - p)
        time_grad = jnp.where(last, 0.0, following[here, :] - p)
        old, old_x, old_y = density[here, :], flux_x[here, :], flux_y[here, :]
        new, new_x, new_y = proximal(old, old_x, old_y, time_grad, grad_x, grad_y, cost[here, :])
        outs[0][here, :] = new
        outs[1][here, :] = new_x
        outs[2][here, :] = new_y
        bar = 2.0 * new - old
        bar_x = 2.0 * new_x - old_x
        bar_y = jnp.where(col == cols - 1, 0.0, 2.0 * new_y - old_y)
        div_y = bar_y - jnp.where(col == 0, 0.0, pltpu.roll(bar_y, 1, 1))
        bar_x = jnp.where(row + r0 == rows - 1, 0.0, bar_x)
        before = jnp.where(row == 0, carry, pltpu.roll(bar_x, 1, 0))
        start = jnp.where(first, init[here, :], 0.0)
        work[1, here, :] = bar
        work[0, here, :] = bar - start + div_y + (bar_x - before)
        return bar_x[TILE - 1 : TILE, :]

    lax.fori_loop(0, rows // TILE, tile, jnp.zeros((1, cols), F32))

    for part in range(2):
        def read(r0, step):
            return work[part, r0 : r0 + step, :]

        def write(r0, step, value):
            hat[part, r0 : r0 + step, :] = value

        two_sided(read, table_x, table_yt, mid, write, rows)


def backward_half(modes, part, pot, table_xt, table_y, out, mid):
    def read(r0, step):
        return modes[part, r0 : r0 + step, :]

    def write(r0, step, value):
        here = slice(r0, r0 + step)
        out[here, :] = pot[here, :] + DUAL_STEP * value

    two_sided(read, table_xt, table_y, mid, write, pot.shape[0])


def factors(n, me, mu_ref, coef, other):
    half, cols = coef.shape[1:]
    quarter = half // 2
    core, side, chip = lax.rem(me, 2), lax.rem(me // 2, 2), me // 2
    ends = chip == n // 2 - 1

    def roots(row):
        mu = mu_ref[pl.ds(pl.multiple_of(row, TILE), TILE), :]
        r = 2.0 / (mu + 2.0 + jnp.sqrt(mu * (mu + 4.0)))
        return mu, r, r * r, jnp.log(r)

    def three(i, r, r2, log_r):
        power = jnp.exp(log_r * (2 * i + 1).astype(F32))
        terms = []
        for _ in range(4):
            terms.append(1.0 + power)
            power = power * r2
        return [r * terms[j] / terms[j + 1] for j in range(3)]

    def main(k, c):
        mu, r, r2, log_r = roots(core * half + k * TILE)
        here = pl.ds(pl.multiple_of(k * TILE, TILE), TILE)
        before, f0, f1 = three(2 * chip - 1, r, r2, log_r)
        h2, h1, h0 = three(n - 3 - 2 * chip, r, r2, log_r)
        g0 = 1.0 / (mu + 2.0 - before - h1)
        for j, value in enumerate((f0, f1, h0, h1, jnp.where(ends, 0.0, h2), g0)):
            coef[j, here, :] = value
        return c

    lax.fori_loop(0, half // TILE, main, 0)

    def rest(k, c):
        _, r, r2, log_r = roots(core * half + side * quarter + k * TILE)
        here = pl.ds(pl.multiple_of(k * TILE, TILE), TILE)
        j0 = 2 * (chip + 1 - 2 * side)
        for part, i in enumerate((j0, n - 2 - j0)):
            one, two, _ = three(i, r, r2, log_r)
            other[part, here, :] = one * two
        return c

    lax.fori_loop(0, quarter // TILE, rest, 0)


def first_kernel(n, *refs):
    sources, (o_d, o_x, o_y, hat, following, coef, other) = refs[:9], refs[9:16]
    work, mid, send, recv, load = refs[16:21]
    held = refs[21:]
    loads = [pltpu.make_async_copy(sources[j], held[j], load.at[j]) for j in range(9)]
    for j in (8, 3, 0, 1, 2, 4, 5, 6, 7):
        loads[j].start()
    density, flux_x, flux_y, _, cost, init, tx, tyt, mu = held
    pot = sources[3]
    me = lax.axis_index("tm")
    chunks = pot.shape[0] // TILE
    barrier = pltpu.get_barrier_semaphore()

    @pl.when(me > 0)
    def _():
        pl.semaphore_signal(barrier, inc=1, device_id={"tm": me - 1}, device_id_type=pl.DeviceIdType.MESH)

    @pl.when(me < n - 1)
    def _():
        pl.semaphore_signal(barrier, inc=1, device_id={"tm": me + 1}, device_id_type=pl.DeviceIdType.MESH)

    @pl.when(me == n - 1)
    def _():
        following[...] = jnp.zeros_like(following)

    pl.semaphore_wait(barrier, (me > 0).astype(jnp.int32) + (me < n - 1).astype(jnp.int32))

    def copy(k):
        here = pl.ds(pl.multiple_of(k * TILE, TILE), TILE)
        return pltpu.make_async_remote_copy(
            src_ref=pot.at[here, :], dst_ref=following.at[here, :], send_sem=send.at[k], recv_sem=recv.at[k],
            device_id={"tm": me - 1}, device_id_type=pl.DeviceIdType.MESH,
        )

    @pl.when(me > 0)
    def _():
        lax.fori_loop(0, chunks, lambda k, c: (copy(k).start(), c)[1], 0)

    loads[8].wait()
    factors(n, me, mu, coef, other)
    for j in range(8):
        loads[j].wait()

    def ready(k):
        @pl.when(me < n - 1)
        def _():
            copy(k).wait_recv()

    forward_half(
        me == 0, me == n - 1, (density, flux_x, flux_y), held[3], following, cost, init, tx, tyt,
        (o_d, o_x, o_y), hat, work, mid, ready,
    )

    @pl.when(me > 0)
    def _():
        lax.fori_loop(0, chunks, lambda k, c: (copy(k).wait_send(), c)[1], 0)


def middle_kernel(
    flag, modes, density, flux_x, flux_y, pot, following, cost, init, tx, txt, ty, tyt,
    o_d, o_x, o_y, o_p, hat, work, mid, moved,
):
    backward_half(modes, 0, pot, txt, ty, o_p, mid)
    backward_half(modes, 1, following, txt, ty, moved, mid)
    first, last = flag[0] == 1, flag[1] == 1
    forward_half(first, last, (density, flux_x, flux_y), o_p, moved, cost, init, tx, tyt, (o_d, o_x, o_y), hat, work, mid)


def last_kernel(modes, pot, txt, ty, o_p, mid):
    backward_half(modes, 0, pot, txt, ty, o_p, mid)


def solve_kernel(
    n, wd, coef, other, x, wd_in, ab_out, ab_in, ab_own, p_in, p_out, q_in, q_out, give, got, own, x_out,
    core_s, core_r, y_s, y_r, p_s, p_r, q_s, q_r, ret_s, ret_r, x_s, x_r,
):
    me = lax.axis_index("tm")
    core = lax.rem(me, 2)
    side = lax.rem(me // 2, 2)
    g = me // 4
    groups = n // 4
    mate = me + 1 - 2 * core
    across = me + 2 - 4 * side
    ahead, behind = me + 4, me - 4
    half = wd.shape[1] // 2
    quarter = half // 2
    rows = quarter // CHUNKS
    cols = wd.shape[2]

    barrier = pltpu.get_barrier_semaphore()
    pl.semaphore_signal(barrier, inc=1, device_id={"tm": mate}, device_id_type=pl.DeviceIdType.MESH)
    pl.semaphore_signal(barrier, inc=1, device_id={"tm": across}, device_id_type=pl.DeviceIdType.MESH)

    @pl.when(g > 0)
    def _():
        pl.semaphore_signal(barrier, inc=1, device_id={"tm": behind}, device_id_type=pl.DeviceIdType.MESH)

    @pl.when(g < groups - 1)
    def _():
        pl.semaphore_signal(barrier, inc=1, device_id={"tm": ahead}, device_id_type=pl.DeviceIdType.MESH)

    @pl.when(g == 0)
    def _():
        p_in[...] = jnp.zeros_like(p_in)

    @pl.when(g == groups - 1)
    def _():
        q_in[...] = jnp.zeros_like(q_in)

    peers = 2 + (g > 0).astype(jnp.int32) + (g < groups - 1).astype(jnp.int32)
    pl.semaphore_wait(barrier, peers)

    def remote(src, dst, send, recv, target):
        return pltpu.make_async_remote_copy(
            src_ref=src, dst_ref=dst, send_sem=send, recv_sem=recv,
            device_id={"tm": target}, device_id_type=pl.DeviceIdType.MESH,
        )

    def at(k):
        return pl.ds(pl.multiple_of(k * rows, rows), rows)

    def in_half(k):
        part = jnp.where(k < CHUNKS, 1 - side, side)
        return pl.multiple_of(part * quarter + lax.rem(k, CHUNKS) * rows, rows)

    def core_copy(k):
        src = wd.at[:, pl.ds(pl.multiple_of((1 - core) * half + in_half(k), rows), rows), :]
        return remote(src, wd_in.at[:, pl.ds(in_half(k), rows), :], core_s.at[k], core_r.at[k], mate)

    def y_copy(k):
        return remote(ab_out.at[:, at(k), :], ab_in.at[:, at(k), :], y_s.at[k], y_r.at[k], across)

    def p_copy(k):
        return remote(p_out.at[at(k), :], p_in.at[at(k), :], p_s.at[k], p_r.at[k], ahead)

    def q_copy(k):
        return remote(q_out.at[at(k), :], q_in.at[at(k), :], q_s.at[k], q_r.at[k], behind)

    def ret_copy(part, k):
        return remote(give.at[part, at(k), :], got.at[part, at(k), :], ret_s.at[part, k], ret_r.at[part, k], across)

    def x_copy(k):
        here = pl.ds(in_half(k), rows)
        there = pl.ds(pl.multiple_of(core * half + in_half(k), rows), rows)
        return remote(x_out.at[:, here, :], x.at[:, there, :], x_s.at[k], x_r.at[k], mate)

    def loop(count, body):
        lax.fori_loop(0, count, lambda k, c: (body(k), c)[1], 0)

    loop(2 * CHUNKS, lambda k: core_copy(k).start())

    low = core == 0

    def sources(k):
        here = pl.ds(in_half(k), rows)
        mine = pl.ds(pl.multiple_of(core * half + in_half(k), rows), rows)
        w_a, d_a = wd[0, mine, :], wd[1, mine, :]
        w_b, d_b = wd_in[0, here, :], wd_in[1, here, :]
        w0 = jnp.where(low, w_a, w_b)
        s1 = jnp.where(low, w_b - d_a, w_a - d_b)
        d1 = jnp.where(low, d_b, d_a)
        return w0, s1, d1, [coef[j, here, :] for j in range(6)]

    def carries(k):
        w0, s1, d1, (f0, f1, h0, h1, h2, _) = sources(k)
        return f1 * (s1 + f0 * w0) - d1, h0 * (w0 + h1 * (s1 - h2 * d1))

    def out_chunk(k):
        core_copy(k).wait_recv()
        a, b = carries(k)
        ab_out[0, at(k), :] = a
        ab_out[1, at(k), :] = b
        y_copy(k).start()

    loop(CHUNKS, out_chunk)

    def own_chunk(k):
        core_copy(k + CHUNKS).wait_recv()
        a, b = carries(k + CHUNKS)
        ab_own[0, at(k), :] = a
        ab_own[1, at(k), :] = b

    loop(CHUNKS, own_chunk)

    left = side == 0

    def ordered(part, k, first, second):
        here = pl.ds(in_half(k + CHUNKS), rows)
        mine, theirs = ab_own[part, at(k), :], ab_in[part, at(k), :]
        rate, rate_other = coef[first, here, :] * coef[second, here, :], other[part, at(k), :]
        return (
            jnp.where(left, mine, theirs), jnp.where(left, rate, rate_other),
            jnp.where(left, theirs, mine), jnp.where(left, rate_other, rate),
        )

    def step(s):
        @pl.when(s < CHUNKS)
        def _():
            y_copy(s).wait_recv()

        kp = s - g

        @pl.when((kp >= 0) & (kp < CHUNKS))
        def _():
            @pl.when(g > 0)
            def _():
                p_copy(kp).wait_recv()

            a0, r0, a1, r1 = ordered(0, kp, 0, 1)
            enter = p_in[at(kp), :]
            middle = a0 + r0 * enter

            @pl.when(g < groups - 1)
            def _():
                p_out[at(kp), :] = a1 + r1 * middle
                p_copy(kp).start()

            own[0, at(kp), :] = jnp.where(left, enter, middle)
            give[0, at(kp), :] = jnp.where(left, middle, enter)
            ret_copy(0, kp).start()

        kq = s - (groups - 1 - g)

        @pl.when((kq >= 0) & (kq < CHUNKS))
        def _():
            @pl.when(g < groups - 1)
            def _():
                q_copy(kq).wait_recv()

            b0, r0, b1, r1 = ordered(1, kq, 2, 3)
            enter = q_in[at(kq), :]
            middle = b1 + r1 * enter

            @pl.when(g > 0)
            def _():
                q_out[at(kq), :] = b0 + r0 * middle
                q_copy(kq).start()

            own[1, at(kq), :] = jnp.where(left, middle, enter)
            give[1, at(kq), :] = jnp.where(left, enter, middle)
            ret_copy(1, kq).start()

    loop(CHUNKS + groups - 1, step)

    def finish(k, carry_p, carry_q):
        w0, s1, d1, (f0, f1, h0, h1, h2, g0) = sources(k)
        q2 = carry_q - h2 * d1
        q1 = h1 * (s1 + q2)
        x0 = (w0 + carry_p + q1) * g0
        x1 = h1 * x0 + q1
        x2 = h2 * x1 + q2
        here = pl.ds(in_half(k), rows)
        mine = pl.ds(pl.multiple_of(core * half + in_half(k), rows), rows)
        x[0, mine, :] = jnp.where(low, x0, x1)
        x[1, mine, :] = jnp.where(low, x1, x2)
        x_out[0, here, :] = jnp.where(low, x1, x0)
        x_out[1, here, :] = jnp.where(low, x2, x1)
        x_copy(k).start()

    loop(CHUNKS, lambda k: finish(k + CHUNKS, own[0, at(k), :], own[1, at(k), :]))

    def returned(k):
        ret_copy(0, k).wait_recv()
        ret_copy(1, k).wait_recv()
        finish(k, got[0, at(k), :], got[1, at(k), :])

    loop(CHUNKS, returned)

    def drain(k):
        core_copy(k).wait_send()
        x_copy(k).wait_send()
        x_copy(k).wait_recv()

    loop(2 * CHUNKS, drain)

    def drain_more(k):
        y_copy(k).wait_send()
        ret_copy(0, k).wait_send()
        ret_copy(1, k).wait_send()

        @pl.when(g < groups - 1)
        def _():
            p_copy(k).wait_send()

        @pl.when(g > 0)
        def _():
            q_copy(k).wait_send()

    loop(CHUNKS, drain_more)


def vmem(count):
    return [pl.BlockSpec(memory_space=pltpu.VMEM)] * count


def local_call(kernel, inputs, outs, scratch, flag=None, collective=None):
    specs = vmem(len(inputs))
    if collective is not None:
        specs = [pl.BlockSpec(memory_space=pltpu.HBM)] * len(inputs)
    if flag is not None:
        specs = [pl.BlockSpec(memory_space=pltpu.SMEM)] + specs
        inputs = [flag] + inputs
    params = dict(vmem_limit_bytes=VMEM_BYTES)
    if collective is not None:
        params.update(collective_id=collective, has_side_effects=True)
    return pl.pallas_call(
        kernel,
        out_shape=[jax.ShapeDtypeStruct(shape, F32) for shape in outs],
        in_specs=specs,
        out_specs=vmem(len(outs)),
        scratch_shapes=scratch,
        compiler_params=pltpu.CompilerParams(**params),
    )(*inputs)


def solve(n, wd, coef, other):
    _, rows, cols = wd.shape
    half, quarter = rows // 2, rows // 4
    dma = pltpu.SemaphoreType.DMA
    two = pltpu.VMEM((2, quarter, cols), F32)
    one = pltpu.VMEM((quarter, cols), F32)
    return pl.pallas_call(
        functools.partial(solve_kernel, n),
        out_shape=jax.ShapeDtypeStruct((2, rows, cols), F32),
        in_specs=vmem(3),
        out_specs=pl.BlockSpec(memory_space=pltpu.VMEM),
        scratch_shapes=[
            pltpu.VMEM((2, half, cols), F32), two, two, two, one, one, one, one, two, two, two,
            pltpu.VMEM((2, half, cols), F32),
            dma((2 * CHUNKS,)), dma((2 * CHUNKS,)), dma((CHUNKS,)), dma((CHUNKS,)),
            dma((CHUNKS,)), dma((CHUNKS,)), dma((CHUNKS,)), dma((CHUNKS,)),
            dma((2, CHUNKS)), dma((2, CHUNKS)), dma((2 * CHUNKS,)), dma((2 * CHUNKS,)),
        ],
        compiler_params=pltpu.CompilerParams(
            vmem_limit_bytes=VMEM_BYTES, collective_id=0, has_side_effects=True
        ),
    )(wd, coef, other)


def local(density, flux_x, flux_y, potential, initial_density, running_cost):
    n = lax.axis_size("tm")
    position = lax.axis_index("tm")
    _, rows, cols = density.shape
    shape = (rows, cols)
    mu = jnp.asarray(SCREENING + spectrum(rows)[:, None] + spectrum(cols)[None, :], F32)
    dma = pltpu.SemaphoreType.DMA((rows // TILE,))
    flag = jnp.stack([position == 0, position == n - 1]).astype(jnp.int32)
    tx, ty = cosine_table(rows), cosine_table(cols)
    table_x, table_xt = jnp.asarray(halves(tx)), jnp.asarray(halves(tx.T))
    table_y, table_yt = jnp.asarray(halves(ty)), jnp.asarray(halves(ty.T))
    work = pltpu.VMEM((2, rows, cols), F32)
    mid = pltpu.VMEM((2, rows, cols), BF16)
    three = [shape] * 3
    hat_shape = (2, rows, cols)

    d, fx, fy, hat, following, coef, other = local_call(
        functools.partial(first_kernel, n),
        [density[0], flux_x[0], flux_y[0], potential[0], running_cost, initial_density, table_x, table_yt, mu],
        three + [hat_shape, shape, (6, rows // 2, cols), (2, rows // 4, cols)],
        [work, mid, dma, dma, pltpu.SemaphoreType.DMA((9,))]
        + [pltpu.VMEM(shape, F32)] * 6 + [mid, mid, pltpu.VMEM(shape, F32)],
        collective=1,
    )
    modes = solve(n, hat, coef, other)
    d, fx, fy, pot, hat = local_call(
        middle_kernel,
        [modes, d, fx, fy, potential[0], following, running_cost, initial_density, table_x, table_xt, table_y, table_yt],
        three + [shape, hat_shape], [work, mid, pltpu.VMEM(shape, F32)], flag,
    )
    modes = solve(n, hat, coef, other)
    (pot,) = local_call(last_kernel, [modes, pot, table_xt, table_y], [shape], [mid])
    return (d[None], fx[None], fy[None], pot[None])


def solution(mesh):
    field = P(("grp", "tm"), None, None)
    flat = P("grp", None)
    return jax.shard_map(
        local,
        mesh=mesh,
        in_specs=(field, field, field, field, flat, flat),
        out_specs=(field, field, field, field),
        check_vma=False,
    )
```
